32 devices in a mesh: parts: 2 (over y), wide: 2 (over x), narrow: 8 (over z, core).
Axes of the slice: x: 2, y: 2, z: 4, core: 2. Of those that a mesh axis runs over, the one named last changes fastest.
Arguments:
- tokens: bfloat16 [6144, 5120], P(('parts', 'wide', 'narrow')), parts along dimension 0, may hold values from -6 to 6
- key_grad: bfloat16 [6144, 512], P(('parts', 'wide', 'narrow')), parts along dimension 0, may hold values from -12 to 12
- gain: bfloat16 [5120], replicated, may hold values from 0.099609375 to 1.8984375
- key_codes: bfloat16 [5120, 512], P('narrow'), may hold values from -4 to 4
- code_scales: bfloat16 [5120, 4], P('narrow'), may hold values from 0.0069885254 to 0.027954102
Outputs:
- token_grad: bfloat16 [6144, 5120], P(('parts', 'wide', 'narrow')), parts along dimension 0
- weight_grad: float32 [1024, 5120], P(('parts', 'wide', 'narrow')), parts along dimension 0
The draws below stay inside these ranges and needn't reach their ends.
There are 2 independent parts, one for each index of `parts`. The reference program is written for one: setup_inputs(seed, part) draws one part's arguments, and reference() takes and returns one part's arrays. A program takes and returns all parts, laid end to end along the dimension named above; an argument that names none is the same for every part. Nothing has to cross between parts.
All inputs are finite; a program needn't handle non-finite values.
Results may differ from the reference program's by a relative error of at most 0.005.
Values may be sent and summed in bfloat16 or wider, within the bound.
No kernel may reach another device: no remote copies, remote signals or barrier semaphores. Data moves between devices by JAX's collectives and lax.ppermute only.
A program may use at most 64 MiB of HBM per device.

```python
import math
import jax
import jax.numpy as jnp
from jax import lax

D = 5120
QCOLS = 128
TOK_DEV = 192
KC = 512
TOKENS = 3072
N_WIDE = 2
N_NARROW = 8


def strengthened(result, key, source, target, blocks, factor):
    owner, partner = [(jnp.arange(result.shape[dim]) // (result.shape[dim] // blocks)).reshape([-1 if axis == dim else 1 for axis in range(result.ndim)]) for dim in (source, target)]
    chosen = jax.random.permutation(key, blocks)[partner]
    strong = (owner == chosen) | (owner == (partner + blocks // 2) % blocks)
    return jnp.where(strong, factor * result, result)


def block_levels(rng, shape, pieces, low, high):
    def one(axis_at, parts):
        heights = jax.random.uniform(jax.random.fold_in(jax.random.fold_in(rng, 6), axis_at), (parts,), jnp.float32, low / len(pieces), high / len(pieces))
        return jnp.repeat(jnp.exp(heights), shape[axis_at] // parts).reshape((-1,) + (1,) * (len(shape) - axis_at - 1))

    factor_of = one(*pieces[0])
    for cut in pieces[1:]:
        factor_of = factor_of * one(*cut)
    return factor_of


def gaussian(own_key, extent, spread, limit, cuts=(), kind=jnp.bfloat16):
    factor_of = block_levels(own_key, extent, cuts, -0.22, 0.18) if cuts else 1.0
    array = jax.random.normal(own_key, extent, jnp.float32) * spread * factor_of
    return jnp.minimum(jnp.maximum(array, -limit), limit).astype(kind)


def heavy_noise(key, extent, deviation, bound, cuts, heavy, held_as=jnp.bfloat16):
    entries = deviation * jax.random.normal(key, extent, jnp.float32)
    if cuts:
        entries = entries * block_levels(key, extent, cuts, -0.22, 0.18)
    return jnp.clip(strengthened(entries, jax.random.fold_in(key, 3), *heavy), -bound, bound).astype(held_as)


def setup_inputs(seed: int = 0, part: int = 0) -> dict:
    seeds = jax.random.split(jax.random.key(seed), 6)
    part_keys = jax.random.split(jax.random.fold_in(seeds[5], part), 6)
    tokens = gaussian(part_keys[0], (TOKENS, D), 1.0, 6.0, ((0, 16),))
    key_grad = heavy_noise(part_keys[1], (TOKENS, KC), 2.0, 12.0, ((0, 16),), (0, 1, 16, 2.0))
    gain = jnp.clip(1.0 + 0.18 * jax.random.normal(seeds[2], (D,), jnp.float32), 0.099609375, 1.8984375).astype(jnp.bfloat16)
    key_codes = gaussian(seeds[3], (D, KC), 1.0, 4.0, ((0, 8),))
    code_scales = jnp.clip(jnp.exp(math.log(0.027954102) - 1.3862944 * jax.random.uniform(seeds[4], (D, KC // QCOLS), jnp.float32) ** block_levels(seeds[4], (D, KC // QCOLS), ((0, 8),), -0.2, 0.2)), 0.0069885254, 0.027954102).astype(jnp.bfloat16)
    return {"tokens": tokens, "key_grad": key_grad, "gain": gain, "key_codes": key_codes, "code_scales": code_scales}


def reference(tokens, key_grad, gain, key_codes, code_scales):
    values = tokens.astype(jnp.float32)
    inverse_rms = lax.rsqrt(lax.optimization_barrier(jnp.mean(values * values, axis=1, keepdims=True)) + 1e-06)
    unit_rows = values * inverse_rms
    gain_wide = gain.astype(jnp.float32)
    normed = (unit_rows * gain_wide).astype(jnp.bfloat16)
    weight = (key_codes.astype(jnp.float32) * jnp.repeat(code_scales.astype(jnp.float32), QCOLS, axis=1)).astype(jnp.bfloat16)
    grad_normed = jnp.dot(key_grad, weight.T, preferred_element_type=jnp.float32)
    scaled = grad_normed * gain_wide
    inner_mean = lax.optimization_barrier(jnp.mean(scaled * unit_rows, axis=1, keepdims=True))
    token_grad = (inverse_rms * (scaled - unit_rows * inner_mean)).astype(jnp.bfloat16)
    device_count = N_WIDE * N_NARROW
    grad_blocks = key_grad.reshape(device_count, TOK_DEV, KC)
    normed_blocks = normed.reshape(device_count, TOK_DEV, D)

    def add_term(running, member):
        grad_block, normed_block = member
        term = jnp.dot(grad_block.T, normed_block, preferred_element_type=jnp.float32).astype(jnp.bfloat16)
        return (running + term.astype(jnp.float32), None)
    summed, unused = lax.scan(add_term, jnp.zeros((KC, D), jnp.float32), (grad_blocks, normed_blocks))
    weight_grad = summed / math.sqrt(TOKENS)
    return (token_grad, weight_grad)
```

```python
import functools
import math

import jax
import jax.numpy as jnp
from jax import lax
from jax.experimental import pallas as pl
from jax.experimental.pallas import tpu as pltpu
from jax.sharding import PartitionSpec as P

F32, BF16 = jnp.float32, jnp.bfloat16
EPS = 1e-06
ROWS = 16
NT = (((1,), (1,)), ((), ()))


def general(tokens, key_grad, gain, key_codes, code_scales):
    row_count = tokens.shape[0]
    feature_count = tokens.shape[1]
    key_width = key_codes.shape[1]
    group_cols = key_width // code_scales.shape[1]
    values = tokens.astype(F32)
    inverse_rms = lax.rsqrt(jnp.mean(values * values, axis=1, keepdims=True) + EPS)
    unit_rows = values * inverse_rms
    gain_wide = gain.astype(F32)
    normed = (unit_rows * gain_wide).astype(BF16)
    weight_shard = (
        key_codes.astype(F32) * jnp.repeat(code_scales.astype(F32), group_cols, axis=1)
    ).astype(BF16)
    product = lax.dot_general(
        key_grad,
        lax.all_gather(weight_shard, "narrow", axis=0, tiled=True),
        NT,
        preferred_element_type=F32,
    )
    scaled = product * gain_wide
    inner_mean = jnp.mean(scaled * unit_rows, axis=1, keepdims=True)
    token_grad = (inverse_rms * (scaled - unit_rows * inner_mean)).astype(BF16)
    term = lax.dot_general(
        key_grad, normed, (((0,), (0,)), ((), ())), preferred_element_type=F32
    ).astype(BF16)
    wide_count = lax.axis_size("wide")
    narrow_count = lax.axis_size("narrow")
    column_block = key_width // (wide_count * narrow_count)
    blocks = term.reshape(wide_count, narrow_count, column_block, feature_count)
    received = lax.all_to_all(blocks, "narrow", split_axis=1, concat_axis=1, tiled=True)
    partial_value = jnp.sum(received.astype(F32), axis=1)
    owned = lax.all_to_all(partial_value, "wide", split_axis=0, concat_axis=0, tiled=True)
    summed = jnp.sum(owned, axis=0)
    token_total = row_count * wide_count * narrow_count
    weight_grad = summed / math.sqrt(token_total)
    return (token_grad, weight_grad)


def call(kernel, out_shape, scratch=(), n_in=1, flops=0, nbytes=0, limit=48, name=None):
    vmem = pl.BlockSpec(memory_space=pltpu.VMEM)
    return pl.pallas_call(
        kernel,
        out_shape=out_shape,
        in_specs=[vmem] * n_in,
        out_specs=jax.tree.map(lambda _: vmem, out_shape),
        scratch_shapes=list(scratch),
        compiler_params=pltpu.CompilerParams(vmem_limit_bytes=limit * 2**20),
        cost_estimate=pl.CostEstimate(flops=flops, bytes_accessed=nbytes, transcendentals=0),
        name=name,
    )


def inverse_rms_into(tok_ref, inv_ref, lanes=1280):
    rows, width = tok_ref.shape

    def step(i, carry):
        at = pl.multiple_of(i * ROWS, ROWS)
        total = jnp.zeros((ROWS, 128), F32)
        for j in range(width // lanes):
            v = tok_ref[pl.ds(at, ROWS), j * lanes : (j + 1) * lanes].astype(F32)
            v = v * v
            for k in range(lanes // 128):
                total = total + v[:, k * 128 : (k + 1) * 128]
        mean = jnp.sum(total, axis=1, keepdims=True) * (1.0 / width)
        inv_ref[pl.ds(at, ROWS), :] = jnp.broadcast_to(lax.rsqrt(mean + EPS), (ROWS, 128))
        return carry

    lax.fori_loop(0, rows // ROWS, step, 0)


def decode_kernel(tok_ref, code_ref, scale_ref, inv_ref, sent_ref, kept_ref):
    groups = scale_ref.shape[1]
    cols = code_ref.shape[1] // groups
    side = lax.axis_index("parts")
    half = groups // 2
    scales = scale_ref[...].astype(F32)
    for g in range(groups):
        block = (code_ref[:, g * cols : (g + 1) * cols].astype(F32) * scales[:, g : g + 1]).astype(BF16)
        at = (g % half) * cols

        @pl.when(side == g // half)
        def _():
            sent_ref[:, at : at + cols] = block

        @pl.when(side != g // half)
        def _():
            kept_ref[:, at : at + cols] = block

    inverse_rms_into(tok_ref, inv_ref)


def term_kernel(first, count, tok_a, tok_b, inv_a, kg_a, kg_b, gain_ref, *refs):
    if first == 0:
        sent_ref, kept_ref, inv_b, select_ref, normed, picked = refs
    else:
        inv_b, select_ref, sent_ref, kept_ref, normed = refs
        picked = select_ref
    rows = tok_a.shape[0]
    if first == 0:
        inverse_rms_into(tok_b, inv_b)
        keys = kg_a.shape[1]
        wide, spot = lax.axis_index("wide"), lax.axis_index("narrow")
        z, core = spot // 2, spot % 2
        row = lax.broadcasted_iota(jnp.int32, (256, keys), 0)
        col = lax.broadcasted_iota(jnp.int32, (256, keys), 1)
        group = row // 32
        order = group % 4
        apart = (order % 2) * 2 + order // 2
        target = 256 * jnp.where(group < 4, 1 - wide, wide) + 64 * (apart ^ z) + 32 * core + row % 32
        pick = jnp.where(col == target, 1.0, 0.0).astype(BF16)
        for n, kg in enumerate((kg_a, kg_b)):
            picked[:, n * rows : (n + 1) * rows] = lax.dot_general(
                pick, kg[...], NT, preferred_element_type=F32
            ).astype(BF16)
        select_ref[...] = picked[...]
    gain = gain_ref[:, first : first + count].astype(F32)
    for n, (tok, inv) in enumerate(((tok_a, inv_a), (tok_b, inv_b))):

        def step(i, carry):
            at = pl.multiple_of(i * ROWS, ROWS)
            scale = inv[pl.ds(at, ROWS), :]
            for j in range(0, count, 128):
                v = tok[pl.ds(at, ROWS), first + j : first + j + 128].astype(F32)
                normed[pl.ds(n * rows + at, ROWS), j : j + 128] = (v * scale * gain[:, j : j + 128]).astype(BF16)
            return carry

        lax.fori_loop(0, rows // ROWS, step, 0)
    tile = 512 if count % 512 == 0 else 256
    for j in range(0, count, tile):
        term = jnp.dot(picked[...], normed[:, j : j + tile], preferred_element_type=F32).astype(BF16)
        sent_ref[:, j : j + tile] = term[:128]
        kept_ref[:, j : j + tile] = term[128:]


def product_kernel(blocks, kg_a, kg_b, *refs):
    parts, (own_ref, sent_ref) = refs[: 2 * blocks], refs[2 * blocks :]
    side = lax.axis_index("parts")
    half = kg_a.shape[1] // 2
    near = pl.ds(pl.multiple_of(side * half, half), half)
    far = pl.ds(pl.multiple_of((1 - side) * half, half), half)
    width = parts[0].shape[0]
    for kg, out in ((kg_b, sent_ref), (kg_a, own_ref)):
        a, b = kg[:, near], kg[:, far]
        for n in range(blocks):
            value = lax.dot_general(a, parts[2 * n][...], NT, preferred_element_type=F32)
            value = value + lax.dot_general(b, parts[2 * n + 1][...], NT, preferred_element_type=F32)
            out[:, n * width : (n + 1) * width] = value.astype(out.dtype)


def token_kernel(counts, tok_ref, inv_ref, gain_ref, *refs):
    pieces, (out_ref, scaled_ref) = refs[:-2], refs[-2:]
    rows, width = tok_ref.shape
    spot = lax.axis_index("narrow")
    z, core = spot // 2, spot % 2
    block = width // 8
    table = []
    k = 0
    for p, count in enumerate(counts):
        for n in range(count):
            for m in range(2):
                who = core if m == 0 else 1 - core
                at = pl.multiple_of(block * (2 * (z ^ k) + who), 128)
                table.append((pieces[2 * p + m], n * block, at, (2 * k + m) * block))
            k += 1

    def step(i, carry):
        r = pl.ds(pl.multiple_of(i * ROWS, ROWS), ROWS)
        inv = inv_ref[r, :]
        total = jnp.zeros((ROWS, 128), F32)
        for ref, start, at, keep in table:
            for j in range(0, block, 128):
                scaled = ref[r, start + j : start + j + 128].astype(F32) * gain_ref[:, pl.ds(at + j, 128)].astype(F32)
                scaled_ref[:, keep + j : keep + j + 128] = scaled
                total = total + scaled * (tok_ref[r, pl.ds(at + j, 128)].astype(F32) * inv)
        mean = jnp.sum(total, axis=1, keepdims=True) * (1.0 / width)
        for ref, start, at, keep in table:
            for j in range(0, block, 128):
                unit = tok_ref[r, pl.ds(at + j, 128)].astype(F32) * inv
                out_ref[r, pl.ds(at + j, 128)] = (inv * (scaled_ref[:, keep + j : keep + j + 128] - unit * mean)).astype(BF16)
        return carry

    lax.fori_loop(0, rows // ROWS, step, 0)


def swap_pairs(count, bit):
    return [(i, i ^ bit) for i in range(count)]


def tuned(tokens, key_grad, gain, key_codes, code_scales):
    rows, width = tokens.shape
    keys = key_grad.shape[1]
    S = jax.ShapeDtypeStruct
    swap = lambda a, axis, bit: lax.ppermute(a, axis, swap_pairs(lax.axis_size(axis), bit))
    core = lambda a: swap(a, "narrow", 1)
    near = lambda a: swap(a, "narrow", 2)
    far = lambda a: swap(a, "narrow", 4)
    across = lambda a: swap(a, "wide", 1)
    beside = lambda a: swap(a, "parts", 1)
    gain_row = gain.reshape(1, width)
    shard = key_codes.shape[0]

    tok_b, kg_b = core(tokens), core(key_grad)
    inv_a, unit, rest = call(
        decode_kernel,
        (S((rows, 128), F32), S((shard, keys // 2), BF16), S((shard, keys // 2), BF16)),
        n_in=3, nbytes=4 * 2**20, name="decode",
    )(tokens, key_codes, code_scales)
    unit_1 = near(unit)
    unit_2 = far(unit)

    cut = width // 2
    half = (S((128, cut), BF16),) * 2
    sent_0, kept_0, inv_b, picked = call(
        functools.partial(term_kernel, 0, cut),
        half + (S((rows, 128), F32), S((256, 2 * rows), BF16)),
        scratch=(pltpu.VMEM((2 * rows, cut), BF16), pltpu.VMEM((256, 2 * rows), BF16)),
        n_in=6, flops=2 * 256 * 2 * rows * cut, nbytes=6 * 2**20, name="term_first",
    )(tokens, tok_b, inv_a, key_grad, kg_b, gain_row)
    sent_1, kept_1 = call(
        functools.partial(term_kernel, cut, cut),
        half,
        scratch=(pltpu.VMEM((2 * rows, cut), BF16),),
        n_in=8, flops=2 * 256 * 2 * rows * cut, nbytes=6 * 2**20, name="term_second",
    )(tokens, tok_b, inv_a, key_grad, kg_b, gain_row, inv_b, picked)

    got_0, got_1 = across(sent_0), across(sent_1)
    unit_3 = near(unit_2)
    other_1, other_2, other_3 = beside(unit_1), beside(unit_2), beside(unit_3)

    owned = []
    for kept, got in ((kept_0, got_0), (kept_1, got_1)):
        total = kept.astype(F32) + got.astype(F32)
        got = near(total[64:].astype(BF16))
        total = total[:64] + got.astype(F32)
        got = far(total[32:].astype(BF16))
        owned.append(total[:32] + got.astype(F32))
    weight_grad = jnp.concatenate(owned, axis=1) / math.sqrt(rows * lax.axis_size("wide") * lax.axis_size("narrow"))

    def product(*parts):
        n = len(parts) // 2
        own, sent = call(
            functools.partial(product_kernel, n),
            (S((rows, n * shard), F32), S((rows, n * shard), BF16)),
            n_in=2 + 2 * n, flops=2 * 2 * rows * keys * n * shard, nbytes=4 * 2**20, name="product",
        )(key_grad, kg_b, *parts)
        return own, core(sent)

    most = product(unit, rest, unit_1, other_1, unit_2, other_2)
    last = product(unit_3, other_3)
    token_grad = call(
        functools.partial(token_kernel, (3, 1)),
        S((rows, width), BF16),
        scratch=(pltpu.VMEM((ROWS, width), F32),),
        n_in=7, nbytes=8 * 2**20, name="token_grad",
    )(tokens, inv_a, gain_row, *most, *last)
    return (token_grad, weight_grad)


def solution(mesh):
    sizes = dict(mesh.shape)
    fits = sizes["parts"] == 2 and sizes["wide"] == 2 and sizes["narrow"] == 8
    return jax.shard_map(
        tuned if fits else general,
        mesh=mesh,
        in_specs=(
            P(("parts", "wide", "narrow"), None),
            P(("parts", "wide", "narrow"), None),
            P(),
            P("narrow", None),
            P("narrow", None),
        ),
        out_specs=(P(("parts", "wide", "narrow"), None), P(("parts", "wide", "narrow"), None)),
        check_vma=False,
    )
```

```python
import functools
import math

import jax
import jax.numpy as jnp
from jax import lax
from jax.experimental import pallas as pl
from jax.experimental.pallas import tpu as pltpu
from jax.sharding import PartitionSpec as P

F32, BF16 = jnp.float32, jnp.bfloat16
EPS = 1e-06
ROWS = 16
STAGES = 4
COST_D = 20000000000.0
COST_P = 0
COST_Q = 0
COST_T = 0
DIRECT = False
CUTS = (768, 2304, 2048)
GROUPS = ((2304,), (2048,))
EVENTS = ('u1', 'u2', 'd0', 'u3', 'f1', 'g1', 'F0', 'd2', 'p', 'F1', 'q', 'F2', 't')
NT = (((1,), (1,)), ((), ()))


def general(tokens, key_grad, gain, key_codes, code_scales):
    row_count = tokens.shape[0]
    feature_count = tokens.shape[1]
    key_width = key_codes.shape[1]
    group_cols = key_width // code_scales.shape[1]
    values = tokens.astype(F32)
    inverse_rms = lax.rsqrt(jnp.mean(values * values, axis=1, keepdims=True) + EPS)
    unit_rows = values * inverse_rms
    gain_wide = gain.astype(F32)
    normed = (unit_rows * gain_wide).astype(BF16)
    weight_shard = (
        key_codes.astype(F32) * jnp.repeat(code_scales.astype(F32), group_cols, axis=1)
    ).astype(BF16)
    product = lax.dot_general(
        key_grad,
        lax.all_gather(weight_shard, "narrow", axis=0, tiled=True),
        NT,
        preferred_element_type=F32,
    )
    scaled = product * gain_wide
    inner_mean = jnp.mean(scaled * unit_rows, axis=1, keepdims=True)
    token_grad = (inverse_rms * (scaled - unit_rows * inner_mean)).astype(BF16)
    term = lax.dot_general(
        key_grad, normed, (((0,), (0,)), ((), ())), preferred_element_type=F32
    ).astype(BF16)
    wide_count = lax.axis_size("wide")
    narrow_count = lax.axis_size("narrow")
    column_block = key_width // (wide_count * narrow_count)
    blocks = term.reshape(wide_count, narrow_count, column_block, feature_count)
    received = lax.all_to_all(blocks, "narrow", split_axis=1, concat_axis=1, tiled=True)
    partial_value = jnp.sum(received.astype(F32), axis=1)
    owned = lax.all_to_all(partial_value, "wide", split_axis=0, concat_axis=0, tiled=True)
    summed = jnp.sum(owned, axis=0)
    token_total = row_count * wide_count * narrow_count
    weight_grad = summed / math.sqrt(token_total)
    return (token_grad, weight_grad)


def call(kernel, out_shape, scratch=(), n_in=1, far_in=(), far_out=False, limit=16, flops=0, name=None):
    vmem = pl.BlockSpec(memory_space=pltpu.VMEM)
    anywhere = pl.BlockSpec(memory_space=pltpu.HBM)
    return pl.pallas_call(
        kernel,
        out_shape=out_shape,
        in_specs=[anywhere if i in far_in else vmem for i in range(n_in)],
        out_specs=jax.tree.map(lambda _: anywhere if far_out else vmem, out_shape),
        scratch_shapes=list(scratch),
        compiler_params=pltpu.CompilerParams(vmem_limit_bytes=limit * 2**20),
        cost_estimate=pl.CostEstimate(flops=int(flops), bytes_accessed=0, transcendentals=0),
        name=name,
    )


def fetch(sources, targets, sems):
    copies = [pltpu.make_async_copy(a, b, sems.at[n]) for n, (a, b) in enumerate(zip(sources, targets))]
    for copy in copies:
        copy.start()
    return copies


def arrived(copies):
    for copy in copies:
        copy.wait()


def inverse_rms_into(tok_ref, inv_ref):
    rows, width = tok_ref.shape

    def step(i, carry):
        r = pl.ds(pl.multiple_of(i * ROWS, ROWS), ROWS)
        totals = [jnp.zeros((ROWS, 128), F32)] * 4
        for j in range(width // 128):
            v = tok_ref[r, j * 128 : (j + 1) * 128].astype(F32)
            totals[j % 4] = totals[j % 4] + v * v
        inv_ref[r, :] = (totals[0] + totals[1]) + (totals[2] + totals[3])
        return carry

    lax.fori_loop(0, rows // ROWS, step, 0)
    mean = jnp.sum(inv_ref[...], axis=1, keepdims=True) * (1.0 / width)
    inv_ref[...] = jnp.broadcast_to(lax.rsqrt(mean + EPS), inv_ref.shape)


def decode_kernel(code_hbm, scale_hbm, sent_ref, kept_ref, code_ref, scale_ref, sems):
    arrived(fetch((code_hbm, scale_hbm), (code_ref, scale_ref), sems))
    groups = scale_ref.shape[0]
    cols = code_ref.shape[1] // groups
    side = lax.axis_index("parts")
    half = groups // 2
    scales = scale_ref[...].astype(F32).T
    for g in range(groups):
        block = (code_ref[:, g * cols : (g + 1) * cols].astype(F32) * scales[:, g : g + 1]).astype(BF16)
        at = (g % half) * cols

        @pl.when(side == g // half)
        def _():
            sent_ref[:, at : at + cols] = block

        @pl.when(side != g // half)
        def _():
            kept_ref[:, at : at + cols] = block


def pick_rows(kg_a, kg_b, picked):
    rows, keys = kg_a.shape
    wide, spot = lax.axis_index("wide"), lax.axis_index("narrow")
    z, core = spot // 2, spot % 2
    row = lax.broadcasted_iota(jnp.int32, (256, 1), 0)
    col = lax.broadcasted_iota(jnp.int32, (256, keys), 1)
    group = row // 32
    order = group % 4
    apart = (order % 2) * 2 + order // 2
    target = 256 * jnp.where(group < 4, 1 - wide, wide) + 64 * (apart ^ z) + 32 * core + row % 32
    pick = jnp.where(col == target, 1.0, 0.0).astype(BF16)
    for n, kg in enumerate((kg_a, kg_b)):
        picked[:, n * rows : (n + 1) * rows] = lax.dot_general(pick, kg[...], NT, preferred_element_type=F32).astype(BF16)


def normed_into(tok, inv, gain, first, count, normed, base):
    def step(i, carry):
        at = pl.multiple_of(i * ROWS, ROWS)
        scale = inv[pl.ds(at, ROWS), :]
        for j in range(0, count, 128):
            v = tok[pl.ds(at, ROWS), first + j : first + j + 128].astype(F32)
            g = gain[(first + j) // 128 : (first + j) // 128 + 1, :]
            normed[pl.ds(base + at, ROWS), j : j + 128] = (v * scale * g).astype(BF16)
        return carry

    lax.fori_loop(0, tok.shape[0] // ROWS, step, 0)


def term_into(picked, normed, sent_ref, kept_ref, first):
    count = sent_ref.shape[1]
    tile = 512 if count % 512 == 0 else 256
    for j in range(0, count, tile):
        term = jnp.dot(picked[...], normed[:, first + j : first + j + tile], preferred_element_type=F32).astype(BF16)
        sent_ref[:, j : j + tile] = term[:128]
        kept_ref[:, j : j + tile] = term[128:]


def first_term_kernel(
    tok_hbm, kg_hbm, gain_hbm, tok_b, kg_b, sent_ref, kept_ref, inv_a, inv_b, picked, tok_a, kg_a, normed, gain_ref, gain, sems
):
    rows = tok_b.shape[0]
    small = fetch((kg_hbm, gain_hbm), (kg_a, gain_ref), sems)
    large = fetch((tok_hbm,), (tok_a,), sems.at[2:])
    inverse_rms_into(tok_b, inv_b)
    arrived(small)
    gain[...] = gain_ref[...].astype(F32)
    pick_rows(kg_a, kg_b, picked)
    arrived(large)
    inverse_rms_into(tok_a, inv_a)
    count = sent_ref.shape[1]
    normed_into(tok_a, inv_a, gain, 0, count, normed, 0)
    normed_into(tok_b, inv_b, gain, 0, count, normed, rows)
    term_into(picked, normed, sent_ref, kept_ref, 0)


def more_terms_kernel(first, tok_hbm, gain_hbm, tok_b, inv_a, inv_b, picked, *refs):
    outs, (tok_a, normed, gain_ref, gain, sems) = refs[:-5], refs[-5:]
    rows = tok_b.shape[0]
    small = fetch((gain_hbm,), (gain_ref,), sems)
    large = fetch((tok_hbm,), (tok_a,), sems.at[1:])
    arrived(small)
    gain[...] = gain_ref[...].astype(F32)
    count = normed.shape[1]
    normed_into(tok_b, inv_b, gain, first, count, normed, rows)
    arrived(large)
    normed_into(tok_a, inv_a, gain, first, count, normed, 0)
    at = 0
    for sent_ref, kept_ref in zip(outs[::2], outs[1::2]):
        term_into(picked, normed, sent_ref, kept_ref, at)
        at += sent_ref.shape[1]


def product_kernel(blocks, kg_a, kg_b, *refs):
    parts, (own_ref, sent_ref) = refs[: 2 * blocks], refs[2 * blocks :]
    side = lax.axis_index("parts")
    half = kg_a.shape[1] // 2
    near = pl.ds(pl.multiple_of(side * half, half), half)
    far = pl.ds(pl.multiple_of((1 - side) * half, half), half)
    width = parts[0].shape[0]
    for kg, out in ((kg_b, sent_ref), (kg_a, own_ref)):
        a, b = kg[:, near], kg[:, far]
        for n in range(blocks):
            value = lax.dot_general(a, parts[2 * n][...], NT, preferred_element_type=F32)
            value = value + lax.dot_general(b, parts[2 * n + 1][...], NT, preferred_element_type=F32)
            out[:, n * width : (n + 1) * width] = value.astype(out.dtype)


def token_kernel(counts, tok_hbm, gain_hbm, inv_ref, *refs):
    pieces, (out_hbm, out_ref, scaled_ref, tok_ref, total_ref, gain_ref, gain, sems) = refs[:-8], refs[-8:]
    arrived(fetch((gain_hbm, tok_hbm), (gain_ref, tok_ref), sems))
    rows, width = tok_ref.shape
    gain[...] = gain_ref[...].astype(F32)
    spot = lax.axis_index("narrow")
    z, core = spot // 2, spot % 2
    block = width // 8
    table = []
    k = 0
    for p, count in enumerate(counts):
        for n in range(count):
            for m in range(2):
                who = core if m == 0 else 1 - core
                table.append((pieces[2 * p + m], n * block, 2 * (z ^ k) + who, (2 * k + m) * block))
            k += 1

    def weigh(i, carry):
        r = pl.ds(pl.multiple_of(i * ROWS, ROWS), ROWS)
        totals = [jnp.zeros((ROWS, 128), F32)] * 4
        for ref, start, where, keep in table:
            for j in range(block // 128):
                spot = where * (block // 128) + j
                scaled = ref[r, start + j * 128 : start + j * 128 + 128].astype(F32) * gain[pl.ds(spot, 1), :]
                scaled_ref[r, keep + j * 128 : keep + j * 128 + 128] = scaled
                unit = tok_ref[r, pl.ds(pl.multiple_of(spot * 128, 128), 128)].astype(F32)
                totals[j % 4] = totals[j % 4] + scaled * unit
        total_ref[r, :] = ((totals[0] + totals[1]) + (totals[2] + totals[3])) * inv_ref[r, :]
        return carry

    lax.fori_loop(0, rows // ROWS, weigh, 0)
    mean = jnp.sum(total_ref[...], axis=1, keepdims=True) * (1.0 / width)
    total_ref[...] = jnp.broadcast_to(mean, total_ref.shape)

    def write(i, carry):
        r = pl.ds(pl.multiple_of(i * ROWS, ROWS), ROWS)
        inv = inv_ref[r, :]
        mean = total_ref[r, :]
        for ref, start, where, keep in table:
            for j in range(block // 128):
                lanes = pl.ds(pl.multiple_of((where * (block // 128) + j) * 128, 128), 128)
                unit = tok_ref[r, lanes].astype(F32) * inv
                scaled = scaled_ref[r, keep + j * 128 : keep + j * 128 + 128]
                out_ref[r, lanes] = (inv * (scaled - unit * mean)).astype(BF16)
        return carry

    stage = rows // STAGES
    copies = []
    for n in range(STAGES):
        lax.fori_loop(n * stage // ROWS, (n + 1) * stage // ROWS, write, 0)
        r = pl.ds(n * stage, stage)
        copies.append(pltpu.make_async_copy(out_ref.at[r], out_hbm.at[r], sems.at[2 + n]))
        copies[-1].start()
    arrived(copies)


def swap_pairs(count, bit):
    return [(i, i ^ bit) for i in range(count)]


def after(value, earlier):
    return lax.optimization_barrier((value, earlier))[0]


def tuned(tokens, key_grad, gain, key_codes, code_scales):
    rows, width = tokens.shape
    keys = key_grad.shape[1]
    S = jax.ShapeDtypeStruct
    swap = lambda a, axis, bit: lax.ppermute(a, axis, swap_pairs(lax.axis_size(axis), bit))
    core = lambda a: swap(a, "narrow", 1)
    near = lambda a: swap(a, "narrow", 2)
    far = lambda a: swap(a, "narrow", 4)
    across = lambda a: swap(a, "wide", 1)
    opposite = lambda a: swap(a, "narrow", 6)
    beside = lambda a: swap(a, "parts", 1)
    shard = key_codes.shape[0]

    tok_b, kg_b = core(tokens), core(key_grad)
    unit, rest = call(
        decode_kernel,
        (S((shard, keys // 2), BF16),) * 2,
        scratch=(
            pltpu.VMEM(key_codes.shape, BF16),
            pltpu.VMEM(code_scales.shape[::-1], BF16),
            pltpu.SemaphoreType.DMA((2,)),
        ),
        n_in=2, far_in=(0, 1), flops=COST_D, name="decode",
    )(key_codes, code_scales.T)
    units = {1: near(unit), 2: far(unit)}
    if DIRECT:
        units[3] = opposite(unit)

    gain_row = gain.reshape(width // 128, 128)
    cuts = CUTS
    inv = S((rows, 128), F32)
    gains = pltpu.VMEM((width // 128, 128), BF16), pltpu.VMEM((width // 128, 128), F32)
    whole = pltpu.VMEM((rows, width), BF16)
    *pair, inv_a, inv_b, picked = call(
        first_term_kernel,
        (S((128, cuts[0]), BF16),) * 2 + (inv, inv, S((256, 2 * rows), BF16)),
        scratch=(
            whole,
            pltpu.VMEM((rows, keys), BF16),
            pltpu.VMEM((2 * rows, cuts[0]), BF16),
            *gains,
            pltpu.SemaphoreType.DMA((3,)),
        ),
        n_in=5, far_in=(0, 1, 2), name="first_term",
    )(tokens, key_grad, gain_row, tok_b, after(kg_b, unit))
    pairs, first = pair, cuts[0]
    for group in GROUPS:
        total = sum(group)
        pairs = pairs + list(
            call(
                functools.partial(more_terms_kernel, first),
                tuple(S((128, cut), BF16) for cut in group for _ in range(2)),
                scratch=(whole, pltpu.VMEM((2 * rows, total), BF16), *gains, pltpu.SemaphoreType.DMA((2,))),
                n_in=6, far_in=(0, 1), name="more_terms",
            )(tokens, gain_row, tok_b, inv_a, inv_b, after(picked, pairs[-1]))
        )
        first += total
    sent, kept = pairs[::2], pairs[1::2]

    got = [across(a) for a in sent]
    scale = 1 / math.sqrt(rows * lax.axis_size("wide") * lax.axis_size("narrow"))
    marker = [sent[-1]]

    def then(value):
        return after(value, marker[0])

    def mark(value):
        marker[0] = value
        return value

    def product(cost, *parts):
        n = len(parts) // 2
        own, sent = call(
            functools.partial(product_kernel, n),
            (S((rows, n * shard), F32), S((rows, n * shard), BF16)),
            n_in=2 + 2 * n, flops=cost, name="product",
        )(key_grad, kg_b, *parts)
        return own, mark(sent)

    totals, received, owned = {}, {}, {}

    def fold(n):
        a, b = then((kept[n], got[n]))
        total = a.astype(F32) + b.astype(F32)
        totals[n] = total[:64]
        received[n] = near(mark(total[64:].astype(BF16)))

    def fold_again(n):
        total = totals[n] + then(received[n]).astype(F32)
        totals[n] = total[:32]
        received[n] = far(mark(total[32:].astype(BF16)))

    def spread(n):
        a, b = then((kept[n], got[n]))
        total = a.astype(F32) + b.astype(F32)
        totals[n] = total[:32]
        pieces = mark([total[32 * i : 32 * i + 32].astype(BF16) for i in range(1, 4)])
        received[n] = far(pieces[0]), near(pieces[1]), opposite(pieces[2])

    def finish(n):
        arrived = received[n] if isinstance(received[n], tuple) else (received[n],)
        total = totals[n]
        for a in then(arrived):
            total = total + a.astype(F32)
        owned[n] = mark(total * scale)

    others = {}

    def arrive(k):
        units[k] = mark(then(units[k]))
        others[k] = beside(units[k])
        if k == 2 and not DIRECT:
            units[3] = near(units[k])

    most = last = None
    for event in EVENTS:
        kind, n = event[0], int(event[1:] or 0)
        if kind == "u":
            arrive(n)
        elif kind == "f":
            fold(n)
        elif kind == "g":
            fold_again(n)
        elif kind == "d":
            spread(n)
        elif kind == "p":
            own, other = product(COST_P, *then((unit, rest, units[1], others[1], units[2], others[2])))
            most = own, core(other)
        elif kind == "q":
            own, other = product(COST_Q, *then((units[3], others[3])))
            last = own, core(other)
        elif kind == "F":
            finish(n)
        elif kind == "t":
            token_grad = call(
                functools.partial(token_kernel, (3, 1)),
                S((rows, width), BF16),
                scratch=(
                    whole,
                    pltpu.VMEM((rows, width), F32),
                    whole,
                    pltpu.VMEM((rows, 128), F32),
                    *gains,
                    pltpu.SemaphoreType.DMA((2 + STAGES,)),
                ),
                n_in=7, far_in=(0, 1), far_out=True, flops=COST_T, name="token_grad",
            )(tokens, gain_row, inv_a, *then((most, last))[0], *last)
            mark(token_grad)
    weight_grad = jnp.concatenate([owned[n] for n in range(len(cuts))], axis=1)
    return (token_grad, weight_grad)


def solution(mesh):
    sizes = dict(mesh.shape)
    fits = sizes["parts"] == 2 and sizes["wide"] == 2 and sizes["narrow"] == 8
    return jax.shard_map(
        tuned if fits else general,
        mesh=mesh,
        in_specs=(
            P(("parts", "wide", "narrow"), None),
            P(("parts", "wide", "narrow"), None),
            P(),
            P("narrow", None),
            P("narrow", None),
        ),
        out_specs=(P(("parts", "wide", "narrow"), None), P(("parts", "wide", "narrow"), None)),
        check_vma=False,
    )
```

```python
import functools
import math

import jax
import jax.numpy as jnp
from jax import lax
from jax.experimental import pallas as pl
from jax.experimental.pallas import tpu as pltpu
from jax.sharding import PartitionSpec as P

F32, BF16 = jnp.float32, jnp.bfloat16
EPS = 1e-06
ROWS = 16
STAGES = 4
COST_D = 20000000000.0
COST_P = 0
LATE = (-1, -1)
COST_Q = 0
COST_T = 0
DIRECT = False
CUTS = (768, 2304, 2048)
GROUPS = ((2304,), (2048,))
EVENTS = ('u1', 'u2', 'f0', 'u3', 'g0', 'd1', 'F0', 'd2', 'p', 'F1', 'q', 'F2', 't')
NT = (((1,), (1,)), ((), ()))


def general(tokens, key_grad, gain, key_codes, code_scales):
    row_count = tokens.shape[0]
    feature_count = tokens.shape[1]
    key_width = key_codes.shape[1]
    group_cols = key_width // code_scales.shape[1]
    values = tokens.astype(F32)
    inverse_rms = lax.rsqrt(jnp.mean(values * values, axis=1, keepdims=True) + EPS)
    unit_rows = values * inverse_rms
    gain_wide = gain.astype(F32)
    normed = (unit_rows * gain_wide).astype(BF16)
    weight_shard = (
        key_codes.astype(F32) * jnp.repeat(code_scales.astype(F32), group_cols, axis=1)
    ).astype(BF16)
    product = lax.dot_general(
        key_grad,
        lax.all_gather(weight_shard, "narrow", axis=0, tiled=True),
        NT,
        preferred_element_type=F32,
    )
    scaled = product * gain_wide
    inner_mean = jnp.mean(scaled * unit_rows, axis=1, keepdims=True)
    token_grad = (inverse_rms * (scaled - unit_rows * inner_mean)).astype(BF16)
    term = lax.dot_general(
        key_grad, normed, (((0,), (0,)), ((), ())), preferred_element_type=F32
    ).astype(BF16)
    wide_count = lax.axis_size("wide")
    narrow_count = lax.axis_size("narrow")
    column_block = key_width // (wide_count * narrow_count)
    blocks = term.reshape(wide_count, narrow_count, column_block, feature_count)
    received = lax.all_to_all(blocks, "narrow", split_axis=1, concat_axis=1, tiled=True)
    partial_value = jnp.sum(received.astype(F32), axis=1)
    owned = lax.all_to_all(partial_value, "wide", split_axis=0, concat_axis=0, tiled=True)
    summed = jnp.sum(owned, axis=0)
    token_total = row_count * wide_count * narrow_count
    weight_grad = summed / math.sqrt(token_total)
    return (token_grad, weight_grad)


def call(kernel, out_shape, scratch=(), n_in=1, far_in=(), far_out=False, limit=16, flops=0, name=None):
    vmem = pl.BlockSpec(memory_space=pltpu.VMEM)
    anywhere = pl.BlockSpec(memory_space=pltpu.HBM)
    return pl.pallas_call(
        kernel,
        out_shape=out_shape,
        in_specs=[anywhere if i in far_in else vmem for i in range(n_in)],
        out_specs=jax.tree.map(lambda _: anywhere if far_out else vmem, out_shape),
        scratch_shapes=list(scratch),
        compiler_params=pltpu.CompilerParams(vmem_limit_bytes=limit * 2**20),
        cost_estimate=pl.CostEstimate(flops=int(flops), bytes_accessed=0, transcendentals=0),
        name=name,
    )


def fetch(sources, targets, sems):
    copies = [pltpu.make_async_copy(a, b, sems.at[n]) for n, (a, b) in enumerate(zip(sources, targets))]
    for copy in copies:
        copy.start()
    return copies


def arrived(copies):
    for copy in copies:
        copy.wait()


def inverse_rms_into(tok_ref, inv_ref):
    rows, width = tok_ref.shape

    def step(i, carry):
        r = pl.ds(pl.multiple_of(i * ROWS, ROWS), ROWS)
        totals = [jnp.zeros((ROWS, 128), F32)] * 4
        for j in range(width // 128):
            v = tok_ref[r, j * 128 : (j + 1) * 128].astype(F32)
            totals[j % 4] = totals[j % 4] + v * v
        inv_ref[r, :] = (totals[0] + totals[1]) + (totals[2] + totals[3])
        return carry

    lax.fori_loop(0, rows // ROWS, step, 0)
    mean = jnp.sum(inv_ref[...], axis=1, keepdims=True) * (1.0 / width)
    inv_ref[...] = jnp.broadcast_to(lax.rsqrt(mean + EPS), inv_ref.shape)


def decode_kernel(code_hbm, scale_hbm, sent_ref, kept_ref, code_ref, scale_ref, sems):
    arrived(fetch((code_hbm, scale_hbm), (code_ref, scale_ref), sems))
    groups = scale_ref.shape[0]
    cols = code_ref.shape[1] // groups
    side = lax.axis_index("parts")
    half = groups // 2
    scales = scale_ref[...].astype(F32).T
    for g in range(groups):
        block = (code_ref[:, g * cols : (g + 1) * cols].astype(F32) * scales[:, g : g + 1]).astype(BF16)
        at = (g % half) * cols

        @pl.when(side == g // half)
        def _():
            sent_ref[:, at : at + cols] = block

        @pl.when(side != g // half)
        def _():
            kept_ref[:, at : at + cols] = block


def pick_rows(kg_a, kg_b, picked):
    rows, keys = kg_a.shape
    wide, spot = lax.axis_index("wide"), lax.axis_index("narrow")
    z, core = spot // 2, spot % 2
    row = lax.broadcasted_iota(jnp.int32, (256, 1), 0)
    col = lax.broadcasted_iota(jnp.int32, (256, keys), 1)
    group = row // 32
    order = group % 4
    apart = (order % 2) * 2 + order // 2
    target = 256 * jnp.where(group < 4, 1 - wide, wide) + 64 * (apart ^ z) + 32 * core + row % 32
    pick = jnp.where(col == target, 1.0, 0.0).astype(BF16)
    for n, kg in enumerate((kg_a, kg_b)):
        picked[:, n * rows : (n + 1) * rows] = lax.dot_general(pick, kg[...], NT, preferred_element_type=F32).astype(BF16)


def normed_into(tok, inv, gain, first, count, normed, base):
    def step(i, carry):
        at = pl.multiple_of(i * ROWS, ROWS)
        scale = inv[pl.ds(at, ROWS), :]
        for j in range(0, count, 128):
            v = tok[pl.ds(at, ROWS), first + j : first + j + 128].astype(F32)
            g = gain[(first + j) // 128 : (first + j) // 128 + 1, :]
            normed[pl.ds(base + at, ROWS), j : j + 128] = (v * scale * g).astype(BF16)
        return carry

    lax.fori_loop(0, tok.shape[0] // ROWS, step, 0)


def term_into(picked, normed, sent_ref, kept_ref, first):
    count = sent_ref.shape[1]
    tile = 512 if count % 512 == 0 else 256
    for j in range(0, count, tile):
        term = jnp.dot(picked[...], normed[:, first + j : first + j + tile], preferred_element_type=F32).astype(BF16)
        sent_ref[:, j : j + tile] = term[:128]
        kept_ref[:, j : j + tile] = term[128:]


def first_term_kernel(
    tok_hbm, kg_hbm, gain_hbm, tok_b, kg_b, sent_ref, kept_ref, inv_a, inv_b, picked, tok_a, kg_a, normed, gain_ref, gain, sems
):
    rows = tok_b.shape[0]
    small = fetch((kg_hbm, gain_hbm), (kg_a, gain_ref), sems)
    large = fetch((tok_hbm,), (tok_a,), sems.at[2:])
    inverse_rms_into(tok_b, inv_b)
    arrived(small)
    gain[...] = gain_ref[...].astype(F32)
    pick_rows(kg_a, kg_b, picked)
    arrived(large)
    inverse_rms_into(tok_a, inv_a)
    count = sent_ref.shape[1]
    normed_into(tok_a, inv_a, gain, 0, count, normed, 0)
    normed_into(tok_b, inv_b, gain, 0, count, normed, rows)
    term_into(picked, normed, sent_ref, kept_ref, 0)


def more_terms_kernel(first, tok_hbm, gain_hbm, tok_b, inv_a, inv_b, picked, *refs):
    outs, (tok_a, normed, gain_ref, gain, sems) = refs[:-5], refs[-5:]
    rows = tok_b.shape[0]
    small = fetch((gain_hbm,), (gain_ref,), sems)
    large = fetch((tok_hbm,), (tok_a,), sems.at[1:])
    arrived(small)
    gain[...] = gain_ref[...].astype(F32)
    count = normed.shape[1]
    normed_into(tok_b, inv_b, gain, first, count, normed, rows)
    arrived(large)
    normed_into(tok_a, inv_a, gain, first, count, normed, 0)
    at = 0
    for sent_ref, kept_ref in zip(outs[::2], outs[1::2]):
        term_into(picked, normed, sent_ref, kept_ref, at)
        at += sent_ref.shape[1]


def product_kernel(blocks, kg_a, kg_b, *refs):
    parts, (own_ref, sent_ref) = refs[: 2 * blocks], refs[2 * blocks :]
    side = lax.axis_index("parts")
    half = kg_a.shape[1] // 2
    near = pl.ds(pl.multiple_of(side * half, half), half)
    far = pl.ds(pl.multiple_of((1 - side) * half, half), half)
    width = parts[0].shape[0]
    for kg, out in ((kg_b, sent_ref), (kg_a, own_ref)):
        a, b = kg[:, near], kg[:, far]
        for n in range(blocks):
            value = lax.dot_general(a, parts[2 * n][...], NT, preferred_element_type=F32)
            value = value + lax.dot_general(b, parts[2 * n + 1][...], NT, preferred_element_type=F32)
            out[:, n * width : (n + 1) * width] = value.astype(out.dtype)


def token_kernel(counts, chunks, tok_hbm, gain_hbm, inv_ref, *refs):
    owned, pieces = refs[:chunks], refs[chunks:-9]
    out_hbm, weight_hbm, out_ref, scaled_ref, tok_ref, total_ref, gain_ref, gain, sems = refs[-9:]
    copies, first = [], 0
    for n, chunk in enumerate(owned):
        target = weight_hbm.at[:, pl.ds(first, chunk.shape[1])]
        copies.append(pltpu.make_async_copy(chunk, target, sems.at[2 + STAGES + n]))
        copies[-1].start()
        first += chunk.shape[1]
    arrived(fetch((gain_hbm, tok_hbm), (gain_ref, tok_ref), sems))
    rows, width = tok_ref.shape
    gain[...] = gain_ref[...].astype(F32)
    spot = lax.axis_index("narrow")
    z, core = spot // 2, spot % 2
    block = width // 8
    table = []
    k = 0
    for p, count in enumerate(counts):
        for n in range(count):
            for m in range(2):
                who = core if m == 0 else 1 - core
                table.append((pieces[2 * p + m], n * block, 2 * (z ^ k) + who, (2 * k + m) * block))
            k += 1

    def weigh(i, carry):
        r = pl.ds(pl.multiple_of(i * ROWS, ROWS), ROWS)
        totals = [jnp.zeros((ROWS, 128), F32)] * 4
        for ref, start, where, keep in table:
            for j in range(block // 128):
                spot = where * (block // 128) + j
                scaled = ref[r, start + j * 128 : start + j * 128 + 128].astype(F32) * gain[pl.ds(spot, 1), :]
                scaled_ref[r, keep + j * 128 : keep + j * 128 + 128] = scaled
                unit = tok_ref[r, pl.ds(pl.multiple_of(spot * 128, 128), 128)].astype(F32)
                totals[j % 4] = totals[j % 4] + scaled * unit
        total_ref[r, :] = ((totals[0] + totals[1]) + (totals[2] + totals[3])) * inv_ref[r, :]
        return carry

    lax.fori_loop(0, rows // ROWS, weigh, 0)
    mean = jnp.sum(total_ref[...], axis=1, keepdims=True) * (1.0 / width)
    total_ref[...] = jnp.broadcast_to(mean, total_ref.shape)

    def write(i, carry):
        r = pl.ds(pl.multiple_of(i * ROWS, ROWS), ROWS)
        inv = inv_ref[r, :]
        mean = total_ref[r, :]
        for ref, start, where, keep in table:
            for j in range(block // 128):
                lanes = pl.ds(pl.multiple_of((where * (block // 128) + j) * 128, 128), 128)
                unit = tok_ref[r, lanes].astype(F32) * inv
                scaled = scaled_ref[r, keep + j * 128 : keep + j * 128 + 128]
                out_ref[r, lanes] = (inv * (scaled - unit * mean)).astype(BF16)
        return carry

    stage = rows // STAGES
    for n in range(STAGES):
        lax.fori_loop(n * stage // ROWS, (n + 1) * stage // ROWS, write, 0)
        r = pl.ds(n * stage, stage)
        copies.append(pltpu.make_async_copy(out_ref.at[r], out_hbm.at[r], sems.at[2 + n]))
        copies[-1].start()
    arrived(copies)


def swap_pairs(count, bit):
    return [(i, i ^ bit) for i in range(count)]


def after(value, earlier):
    return lax.optimization_barrier((value, earlier))[0]


def tuned(tokens, key_grad, gain, key_codes, code_scales):
    rows, width = tokens.shape
    keys = key_grad.shape[1]
    S = jax.ShapeDtypeStruct
    swap = lambda a, axis, bit: lax.ppermute(a, axis, swap_pairs(lax.axis_size(axis), bit))
    core = lambda a: swap(a, "narrow", 1)
    near = lambda a: swap(a, "narrow", 2)
    far = lambda a: swap(a, "narrow", 4)
    across = lambda a: swap(a, "wide", 1)
    opposite = lambda a: swap(a, "narrow", 6)
    beside = lambda a: swap(a, "parts", 1)
    shard = key_codes.shape[0]

    tok_b, kg_b = core(tokens), core(key_grad)
    unit, rest = call(
        decode_kernel,
        (S((shard, keys // 2), BF16),) * 2,
        scratch=(
            pltpu.VMEM(key_codes.shape, BF16),
            pltpu.VMEM(code_scales.shape[::-1], BF16),
            pltpu.SemaphoreType.DMA((2,)),
        ),
        n_in=2, far_in=(0, 1), flops=COST_D, name="decode",
    )(key_codes, code_scales.T)

    gain_row = gain.reshape(width // 128, 128)
    cuts = CUTS
    inv = S((rows, 128), F32)
    gains = pltpu.VMEM((width // 128, 128), BF16), pltpu.VMEM((width // 128, 128), F32)
    whole = pltpu.VMEM((rows, width), BF16)
    *pair, inv_a, inv_b, picked = call(
        first_term_kernel,
        (S((128, cuts[0]), BF16),) * 2 + (inv, inv, S((256, 2 * rows), BF16)),
        scratch=(
            whole,
            pltpu.VMEM((rows, keys), BF16),
            pltpu.VMEM((2 * rows, cuts[0]), BF16),
            *gains,
            pltpu.SemaphoreType.DMA((3,)),
        ),
        n_in=5, far_in=(0, 1, 2), name="first_term",
    )(tokens, key_grad, gain_row, tok_b, after(kg_b, unit))
    pairs, first = pair, cuts[0]
    for group in GROUPS:
        total = sum(group)
        pairs = pairs + list(
            call(
                functools.partial(more_terms_kernel, first),
                tuple(S((128, cut), BF16) for cut in group for _ in range(2)),
                scratch=(whole, pltpu.VMEM((2 * rows, total), BF16), *gains, pltpu.SemaphoreType.DMA((2,))),
                n_in=6, far_in=(0, 1), name="more_terms",
            )(tokens, gain_row, tok_b, inv_a, inv_b, after(picked, pairs[-1]))
        )
        first += total
    sent, kept = pairs[::2], pairs[1::2]

    units = {k: move(after(unit, sent[n]) if n >= 0 else unit) for k, move, n in ((1, near, LATE[0]), (2, far, LATE[1]))}
    if DIRECT:
        units[3] = opposite(unit)
    got = [across(a) for a in sent]
    scale = 1 / math.sqrt(rows * lax.axis_size("wide") * lax.axis_size("narrow"))
    marker = [sent[-1]]

    def then(value):
        return after(value, marker[0])

    def mark(value):
        marker[0] = value
        return value

    def product(cost, *parts):
        n = len(parts) // 2
        own, sent = call(
            functools.partial(product_kernel, n),
            (S((rows, n * shard), F32), S((rows, n * shard), BF16)),
            n_in=2 + 2 * n, flops=cost, name="product",
        )(key_grad, kg_b, *parts)
        return own, mark(sent)

    totals, received, owned = {}, {}, {}

    def fold(n):
        a, b = then((kept[n], got[n]))
        total = a.astype(F32) + b.astype(F32)
        totals[n] = total[:64]
        received[n] = near(mark(total[64:].astype(BF16)))

    def fold_again(n):
        total = totals[n] + then(received[n]).astype(F32)
        totals[n] = total[:32]
        received[n] = far(mark(total[32:].astype(BF16)))

    def spread(n):
        a, b = then((kept[n], got[n]))
        total = a.astype(F32) + b.astype(F32)
        totals[n] = total[:32]
        pieces = mark([total[32 * i : 32 * i + 32].astype(BF16) for i in range(1, 4)])
        received[n] = far(pieces[0]), near(pieces[1]), opposite(pieces[2])

    def finish(n):
        arrived = received[n] if isinstance(received[n], tuple) else (received[n],)
        total = totals[n]
        for a in then(arrived):
            total = total + a.astype(F32)
        owned[n] = mark(total * scale)

    others = {}

    def arrive(k):
        units[k] = mark(then(units[k]))
        others[k] = beside(units[k])
        if k == 2 and not DIRECT:
            units[3] = near(units[k])

    most = last = None
    for event in EVENTS:
        kind, n = event[0], int(event[1:] or 0)
        if kind == "u":
            arrive(n)
        elif kind == "f":
            fold(n)
        elif kind == "g":
            fold_again(n)
        elif kind == "d":
            spread(n)
        elif kind == "p":
            own, other = product(COST_P, *then((unit, rest, units[1], others[1], units[2], others[2])))
            most = own, core(other)
        elif kind == "q":
            own, other = product(COST_Q, *then((units[3], others[3])))
            last = own, core(other)
        elif kind == "F":
            finish(n)
        elif kind == "t":
            token_grad, weight_grad = call(
                functools.partial(token_kernel, (3, 1), len(cuts)),
                (S((rows, width), BF16), S((32, width), F32)),
                scratch=(
                    whole,
                    pltpu.VMEM((rows, width), F32),
                    whole,
                    pltpu.VMEM((rows, 128), F32),
                    *gains,
                    pltpu.SemaphoreType.DMA((2 + STAGES + len(cuts),)),
                ),
                n_in=7 + len(cuts), far_in=(0, 1), far_out=True, flops=COST_T, name="token_grad",
            )(tokens, gain_row, inv_a, *then([owned[n] for n in range(len(cuts))]), *most, *last)
    return (token_grad, weight_grad)


def solution(mesh):
    sizes = dict(mesh.shape)
    fits = sizes["parts"] == 2 and sizes["wide"] == 2 and sizes["narrow"] == 8
    return jax.shard_map(
        tuned if fits else general,
        mesh=mesh,
        in_specs=(
            P(("parts", "wide", "narrow"), None),
            P(("parts", "wide", "narrow"), None),
            P(),
            P("narrow", None),
            P("narrow", None),
        ),
        out_specs=(P(("parts", "wide", "narrow"), None), P(("parts", "wide", "narrow"), None)),
        check_vma=False,
    )
```

```python
import functools
import math

import jax
import jax.numpy as jnp
from jax import lax
from jax.experimental import pallas as pl
from jax.experimental.pallas import tpu as pltpu
from jax.sharding import PartitionSpec as P

F32, BF16 = jnp.float32, jnp.bfloat16
EPS = 1e-06
ROWS = 16
STAGES = 4
COST_D = 20000000000.0
COST_P = 0
LATE = (-1, -1)
COST_Q = 0
COST_T = 0
DIRECT = False
CUTS = (768, 2304, 2048)
GROUPS = ((2304,), (2048,))
EVENTS = ('u1', 'u2', 'f0', 'u3', 'g0', 'd1', 'F0', 'd2', 'p', 'F1', 'q', 'F2', 't')
NT = (((1,), (1,)), ((), ()))


def general(tokens, key_grad, gain, key_codes, code_scales):
    row_count = tokens.shape[0]
    feature_count = tokens.shape[1]
    key_width = key_codes.shape[1]
    group_cols = key_width // code_scales.shape[1]
    values = tokens.astype(F32)
    inverse_rms = lax.rsqrt(jnp.mean(values * values, axis=1, keepdims=True) + EPS)
    unit_rows = values * inverse_rms
    gain_wide = gain.astype(F32)
    normed = (unit_rows * gain_wide).astype(BF16)
    weight_shard = (
        key_codes.astype(F32) * jnp.repeat(code_scales.astype(F32), group_cols, axis=1)
    ).astype(BF16)
    product = lax.dot_general(
        key_grad,
        lax.all_gather(weight_shard, "narrow", axis=0, tiled=True),
        NT,
        preferred_element_type=F32,
    )
    scaled = product * gain_wide
    inner_mean = jnp.mean(scaled * unit_rows, axis=1, keepdims=True)
    token_grad = (inverse_rms * (scaled - unit_rows * inner_mean)).astype(BF16)
    term = lax.dot_general(
        key_grad, normed, (((0,), (0,)), ((), ())), preferred_element_type=F32
    ).astype(BF16)
    wide_count = lax.axis_size("wide")
    narrow_count = lax.axis_size("narrow")
    column_block = key_width // (wide_count * narrow_count)
    blocks = term.reshape(wide_count, narrow_count, column_block, feature_count)
    received = lax.all_to_all(blocks, "narrow", split_axis=1, concat_axis=1, tiled=True)
    partial_value = jnp.sum(received.astype(F32), axis=1)
    owned = lax.all_to_all(partial_value, "wide", split_axis=0, concat_axis=0, tiled=True)
    summed = jnp.sum(owned, axis=0)
    token_total = row_count * wide_count * narrow_count
    weight_grad = summed / math.sqrt(token_total)
    return (token_grad, weight_grad)


def call(kernel, out_shape, scratch=(), n_in=1, far_in=(), far_out=False, limit=16, flops=0, name=None):
    vmem = pl.BlockSpec(memory_space=pltpu.VMEM)
    anywhere = pl.BlockSpec(memory_space=pltpu.HBM)
    return pl.pallas_call(
        kernel,
        out_shape=out_shape,
        in_specs=[anywhere if i in far_in else vmem for i in range(n_in)],
        out_specs=jax.tree.map(lambda _: anywhere if far_out else vmem, out_shape),
        scratch_shapes=list(scratch),
        compiler_params=pltpu.CompilerParams(vmem_limit_bytes=limit * 2**20),
        cost_estimate=pl.CostEstimate(flops=int(flops), bytes_accessed=0, transcendentals=0),
        name=name,
    )


def fetch(sources, targets, sems):
    copies = [pltpu.make_async_copy(a, b, sems.at[n]) for n, (a, b) in enumerate(zip(sources, targets))]
    for copy in copies:
        copy.start()
    return copies


def arrived(copies):
    for copy in copies:
        copy.wait()


def inverse_rms_into(tok_ref, inv_ref):
    rows, width = tok_ref.shape

    def step(i, carry):
        r = pl.ds(pl.multiple_of(i * ROWS, ROWS), ROWS)
        totals = [jnp.zeros((ROWS, 128), F32)] * 4
        for j in range(width // 128):
            v = tok_ref[r, j * 128 : (j + 1) * 128].astype(F32)
            totals[j % 4] = totals[j % 4] + v * v
        inv_ref[r, :] = (totals[0] + totals[1]) + (totals[2] + totals[3])
        return carry

    lax.fori_loop(0, rows // ROWS, step, 0, unroll=2)
    mean = jnp.sum(inv_ref[...], axis=1, keepdims=True) * (1.0 / width)
    inv_ref[...] = jnp.broadcast_to(lax.rsqrt(mean + EPS), inv_ref.shape)


def decode_kernel(code_hbm, scale_hbm, sent_ref, kept_ref, code_ref, scale_ref, sems):
    arrived(fetch((code_hbm, scale_hbm), (code_ref, scale_ref), sems))
    groups = scale_ref.shape[0]
    cols = code_ref.shape[1] // groups
    side = lax.axis_index("parts")
    half = groups // 2
    scales = scale_ref[...].astype(F32).T
    for g in range(groups):
        block = (code_ref[:, g * cols : (g + 1) * cols].astype(F32) * scales[:, g : g + 1]).astype(BF16)
        at = (g % half) * cols

        @pl.when(side == g // half)
        def _():
            sent_ref[:, at : at + cols] = block

        @pl.when(side != g // half)
        def _():
            kept_ref[:, at : at + cols] = block


def pick_rows(kg_a, kg_b, picked):
    rows, keys = kg_a.shape
    wide, spot = lax.axis_index("wide"), lax.axis_index("narrow")
    z, core = spot // 2, spot % 2
    row = lax.broadcasted_iota(jnp.int32, (256, 1), 0)
    col = lax.broadcasted_iota(jnp.int32, (256, keys), 1)
    group = row // 32
    order = group % 4
    apart = (order % 2) * 2 + order // 2
    target = 256 * jnp.where(group < 4, 1 - wide, wide) + 64 * (apart ^ z) + 32 * core + row % 32
    pick = jnp.where(col == target, 1.0, 0.0).astype(BF16)
    for n, kg in enumerate((kg_a, kg_b)):
        picked[:, n * rows : (n + 1) * rows] = lax.dot_general(pick, kg[...], NT, preferred_element_type=F32).astype(BF16)


def normed_into(tok, inv, gain, first, count, normed, base):
    def step(i, carry):
        at = pl.multiple_of(i * ROWS, ROWS)
        scale = inv[pl.ds(at, ROWS), :]
        for j in range(0, count, 128):
            v = tok[pl.ds(at, ROWS), first + j : first + j + 128].astype(F32)
            g = gain[(first + j) // 128 : (first + j) // 128 + 1, :]
            normed[pl.ds(base + at, ROWS), j : j + 128] = (v * scale * g).astype(BF16)
        return carry

    lax.fori_loop(0, tok.shape[0] // ROWS, step, 0, unroll=2)


def term_into(picked, normed, sent_ref, kept_ref, first):
    count = sent_ref.shape[1]
    tile = 512 if count % 512 == 0 else 256
    for j in range(0, count, tile):
        term = jnp.dot(picked[...], normed[:, first + j : first + j + tile], preferred_element_type=F32).astype(BF16)
        sent_ref[:, j : j + tile] = term[:128]
        kept_ref[:, j : j + tile] = term[128:]


def first_term_kernel(
    tok_hbm, kg_hbm, gain_hbm, tok_b, kg_b, sent_ref, kept_ref, inv_a, inv_b, picked, tok_a, kg_a, normed, gain_ref, gain, sems
):
    rows = tok_b.shape[0]
    small = fetch((kg_hbm, gain_hbm), (kg_a, gain_ref), sems)
    large = fetch((tok_hbm,), (tok_a,), sems.at[2:])
    inverse_rms_into(tok_b, inv_b)
    arrived(small)
    gain[...] = gain_ref[...].astype(F32)
    pick_rows(kg_a, kg_b, picked)
    arrived(large)
    inverse_rms_into(tok_a, inv_a)
    count = sent_ref.shape[1]
    normed_into(tok_a, inv_a, gain, 0, count, normed, 0)
    normed_into(tok_b, inv_b, gain, 0, count, normed, rows)
    term_into(picked, normed, sent_ref, kept_ref, 0)


def more_terms_kernel(first, tok_hbm, gain_hbm, tok_b, inv_a, inv_b, picked, *refs):
    outs, (tok_a, normed, gain_ref, gain, sems) = refs[:-5], refs[-5:]
    rows = tok_b.shape[0]
    small = fetch((gain_hbm,), (gain_ref,), sems)
    large = fetch((tok_hbm,), (tok_a,), sems.at[1:])
    arrived(small)
    gain[...] = gain_ref[...].astype(F32)
    count = normed.shape[1]
    normed_into(tok_b, inv_b, gain, first, count, normed, rows)
    arrived(large)
    normed_into(tok_a, inv_a, gain, first, count, normed, 0)
    at = 0
    for sent_ref, kept_ref in zip(outs[::2], outs[1::2]):
        term_into(picked, normed, sent_ref, kept_ref, at)
        at += sent_ref.shape[1]


def product_kernel(blocks, kg_a, kg_b, *refs):
    parts, (own_ref, sent_ref) = refs[: 2 * blocks], refs[2 * blocks :]
    side = lax.axis_index("parts")
    half = kg_a.shape[1] // 2
    near = pl.ds(pl.multiple_of(side * half, half), half)
    far = pl.ds(pl.multiple_of((1 - side) * half, half), half)
    width = parts[0].shape[0]
    for kg, out in ((kg_b, sent_ref), (kg_a, own_ref)):
        a, b = kg[:, near], kg[:, far]
        for n in range(blocks):
            value = lax.dot_general(a, parts[2 * n][...], NT, preferred_element_type=F32)
            value = value + lax.dot_general(b, parts[2 * n + 1][...], NT, preferred_element_type=F32)
            out[:, n * width : (n + 1) * width] = value.astype(out.dtype)


def token_kernel(counts, chunks, tok_hbm, gain_hbm, inv_ref, *refs):
    owned, pieces = refs[:chunks], refs[chunks:-9]
    out_hbm, weight_hbm, out_ref, scaled_ref, tok_ref, total_ref, gain_ref, gain, sems = refs[-9:]
    copies, first = [], 0
    for n, chunk in enumerate(owned):
        target = weight_hbm.at[:, pl.ds(first, chunk.shape[1])]
        copies.append(pltpu.make_async_copy(chunk, target, sems.at[2 + STAGES + n]))
        copies[-1].start()
        first += chunk.shape[1]
    arrived(fetch((gain_hbm, tok_hbm), (gain_ref, tok_ref), sems))
    rows, width = tok_ref.shape
    gain[...] = gain_ref[...].astype(F32)
    spot = lax.axis_index("narrow")
    z, core = spot // 2, spot % 2
    block = width // 8
    table = []
    k = 0
    for p, count in enumerate(counts):
        for n in range(count):
            for m in range(2):
                who = core if m == 0 else 1 - core
                table.append((pieces[2 * p + m], n * block, 2 * (z ^ k) + who, (2 * k + m) * block))
            k += 1

    def weigh(i, carry):
        r = pl.ds(pl.multiple_of(i * ROWS, ROWS), ROWS)
        totals = [jnp.zeros((ROWS, 128), F32)] * 4
        for ref, start, where, keep in table:
            for j in range(block // 128):
                spot = where * (block // 128) + j
                scaled = ref[r, start + j * 128 : start + j * 128 + 128].astype(F32) * gain[pl.ds(spot, 1), :]
                scaled_ref[r, keep + j * 128 : keep + j * 128 + 128] = scaled
                unit = tok_ref[r, pl.ds(pl.multiple_of(spot * 128, 128), 128)].astype(F32)
                totals[j % 4] = totals[j % 4] + scaled * unit
        total_ref[r, :] = ((totals[0] + totals[1]) + (totals[2] + totals[3])) * inv_ref[r, :]
        return carry

    lax.fori_loop(0, rows // ROWS, weigh, 0, unroll=2)
    mean = jnp.sum(total_ref[...], axis=1, keepdims=True) * (1.0 / width)
    total_ref[...] = jnp.broadcast_to(mean, total_ref.shape)

    def write(i, carry):
        r = pl.ds(pl.multiple_of(i * ROWS, ROWS), ROWS)
        inv = inv_ref[r, :]
        mean = total_ref[r, :]
        for ref, start, where, keep in table:
            for j in range(block // 128):
                lanes = pl.ds(pl.multiple_of((where * (block // 128) + j) * 128, 128), 128)
                unit = tok_ref[r, lanes].astype(F32) * inv
                scaled = scaled_ref[r, keep + j * 128 : keep + j * 128 + 128]
                out_ref[r, lanes] = (inv * (scaled - unit * mean)).astype(BF16)
        return carry

    stage = rows // STAGES
    for n in range(STAGES):
        lax.fori_loop(n * stage // ROWS, (n + 1) * stage // ROWS, write, 0, unroll=3)
        r = pl.ds(n * stage, stage)
        copies.append(pltpu.make_async_copy(out_ref.at[r], out_hbm.at[r], sems.at[2 + n]))
        copies[-1].start()
    arrived(copies)


def swap_pairs(count, bit):
    return [(i, i ^ bit) for i in range(count)]


def after(value, earlier):
    return lax.optimization_barrier((value, earlier))[0]


def tuned(tokens, key_grad, gain, key_codes, code_scales):
    rows, width = tokens.shape
    keys = key_grad.shape[1]
    S = jax.ShapeDtypeStruct
    swap = lambda a, axis, bit: lax.ppermute(a, axis, swap_pairs(lax.axis_size(axis), bit))
    core = lambda a: swap(a, "narrow", 1)
    near = lambda a: swap(a, "narrow", 2)
    far = lambda a: swap(a, "narrow", 4)
    across = lambda a: swap(a, "wide", 1)
    opposite = lambda a: swap(a, "narrow", 6)
    beside = lambda a: swap(a, "parts", 1)
    shard = key_codes.shape[0]

    tok_b, kg_b = core(tokens), core(key_grad)
    unit, rest = call(
        decode_kernel,
        (S((shard, keys // 2), BF16),) * 2,
        scratch=(
            pltpu.VMEM(key_codes.shape, BF16),
            pltpu.VMEM(code_scales.shape[::-1], BF16),
            pltpu.SemaphoreType.DMA((2,)),
        ),
        n_in=2, far_in=(0, 1), flops=COST_D, name="decode",
    )(key_codes, code_scales.T)

    gain_row = gain.reshape(width // 128, 128)
    cuts = CUTS
    inv = S((rows, 128), F32)
    gains = pltpu.VMEM((width // 128, 128), BF16), pltpu.VMEM((width // 128, 128), F32)
    whole = pltpu.VMEM((rows, width), BF16)
    *pair, inv_a, inv_b, picked = call(
        first_term_kernel,
        (S((128, cuts[0]), BF16),) * 2 + (inv, inv, S((256, 2 * rows), BF16)),
        scratch=(
            whole,
            pltpu.VMEM((rows, keys), BF16),
            pltpu.VMEM((2 * rows, cuts[0]), BF16),
            *gains,
            pltpu.SemaphoreType.DMA((3,)),
        ),
        n_in=5, far_in=(0, 1, 2), name="first_term",
    )(tokens, key_grad, gain_row, tok_b, after(kg_b, unit))
    pairs, first = pair, cuts[0]
    for group in GROUPS:
        total = sum(group)
        pairs = pairs + list(
            call(
                functools.partial(more_terms_kernel, first),
                tuple(S((128, cut), BF16) for cut in group for _ in range(2)),
                scratch=(whole, pltpu.VMEM((2 * rows, total), BF16), *gains, pltpu.SemaphoreType.DMA((2,))),
                n_in=6, far_in=(0, 1), name="more_terms",
            )(tokens, gain_row, tok_b, inv_a, inv_b, after(picked, pairs[-1]))
        )
        first += total
    sent, kept = pairs[::2], pairs[1::2]

    units = {k: move(after(unit, sent[n]) if n >= 0 else unit) for k, move, n in ((1, near, LATE[0]), (2, far, LATE[1]))}
    if DIRECT:
        units[3] = opposite(unit)
    got = [across(a) for a in sent]
    scale = 1 / math.sqrt(rows * lax.axis_size("wide") * lax.axis_size("narrow"))
    marker = [sent[-1]]

    def then(value):
        return after(value, marker[0])

    def mark(value):
        marker[0] = value
        return value

    def product(cost, *parts):
        n = len(parts) // 2
        own, sent = call(
            functools.partial(product_kernel, n),
            (S((rows, n * shard), F32), S((rows, n * shard), BF16)),
            n_in=2 + 2 * n, flops=cost, name="product",
        )(key_grad, kg_b, *parts)
        return own, mark(sent)

    totals, received, owned = {}, {}, {}

    def fold(n):
        a, b = then((kept[n], got[n]))
        total = a.astype(F32) + b.astype(F32)
        totals[n] = total[:64]
        received[n] = near(mark(total[64:].astype(BF16)))

    def fold_again(n):
        total = totals[n] + then(received[n]).astype(F32)
        totals[n] = total[:32]
        received[n] = far(mark(total[32:].astype(BF16)))

    def spread(n):
        a, b = then((kept[n], got[n]))
        total = a.astype(F32) + b.astype(F32)
        totals[n] = total[:32]
        pieces = mark([total[32 * i : 32 * i + 32].astype(BF16) for i in range(1, 4)])
        received[n] = far(pieces[0]), near(pieces[1]), opposite(pieces[2])

    def finish(n):
        arrived = received[n] if isinstance(received[n], tuple) else (received[n],)
        total = totals[n]
        for a in then(arrived):
            total = total + a.astype(F32)
        owned[n] = mark(total * scale)

    others = {}

    def arrive(k):
        units[k] = mark(then(units[k]))
        others[k] = beside(units[k])
        if k == 2 and not DIRECT:
            units[3] = near(units[k])

    most = last = None
    for event in EVENTS:
        kind, n = event[0], int(event[1:] or 0)
        if kind == "u":
            arrive(n)
        elif kind == "f":
            fold(n)
        elif kind == "g":
            fold_again(n)
        elif kind == "d":
            spread(n)
        elif kind == "p":
            own, other = product(COST_P, *then((unit, rest, units[1], others[1], units[2], others[2])))
            most = own, core(other)
        elif kind == "q":
            own, other = product(COST_Q, *then((units[3], others[3])))
            last = own, core(other)
        elif kind == "F":
            finish(n)
        elif kind == "t":
            token_grad, weight_grad = call(
                functools.partial(token_kernel, (3, 1), len(cuts)),
                (S((rows, width), BF16), S((32, width), F32)),
                scratch=(
                    whole,
                    pltpu.VMEM((rows, width), F32),
                    whole,
                    pltpu.VMEM((rows, 128), F32),
                    *gains,
                    pltpu.SemaphoreType.DMA((2 + STAGES + len(cuts),)),
                ),
                n_in=7 + len(cuts), far_in=(0, 1), far_out=True, flops=COST_T, name="token_grad",
            )(tokens, gain_row, inv_a, *then([owned[n] for n in range(len(cuts))]), *most, *last)
    return (token_grad, weight_grad)


def solution(mesh):
    sizes = dict(mesh.shape)
    fits = sizes["parts"] == 2 and sizes["wide"] == 2 and sizes["narrow"] == 8
    return jax.shard_map(
        tuned if fits else general,
        mesh=mesh,
        in_specs=(
            P(("parts", "wide", "narrow"), None),
            P(("parts", "wide", "narrow"), None),
            P(),
            P("narrow", None),
            P("narrow", None),
        ),
        out_specs=(P(("parts", "wide", "narrow"), None), P(("parts", "wide", "narrow"), None)),
        check_vma=False,
    )
```
